512 devices in a mesh: pair: 128 (over x, z, y_hi), occ: 4 (over y_lo, core).
Axes of the slice: x: 4, y: 4 (y_hi: 2, y_lo: 2; y = y_hi * 2 + y_lo), z: 16, core: 2. Of those that a mesh axis runs over, the one named last changes fastest.
Arguments:
- amplitudes: bfloat16 [128, 768, 4096], P('pair', 'occ'), may hold values from -6 to 6
- integrals: bfloat16 [128, 4096, 512], P('pair', 'occ'), may hold values from -0.03125 to 0.03125
- block_mask: int32 [128], P('pair'), may hold values 0 or 1
Outputs:
- ladder: float32 [768, 512], P('pair', 'occ')
The draws below stay inside these ranges and needn't reach their ends.
All inputs are finite; a program needn't handle non-finite values. No bound on the sum of `block_mask` on one device may be relied on, other than what follows from the above.
Results may differ from the reference program's by a relative error of at most 0.0003.
Values may be sent and summed in bfloat16 or wider, within the bound.
No kernel may reach another device: no remote copies, remote signals or barrier semaphores. Data moves between devices by JAX's collectives and lax.ppermute only.
A program may use at most 64 MiB of HBM per device.

```python
import jax
import jax.numpy as jnp
from jax import lax

TILE = 4096
ROWS = 768
NPB = 128
W_AB = 512


def touch_ends(result, stream_key, least, high):
    dims = result.shape
    place = [jax.random.randint(jax.random.fold_in(stream_key, axis), (), 0, dims[axis]) for axis in range(len(dims))]
    result = result.at[tuple(place)].set(least)
    longest = dims.index(max(dims))
    place[longest] = (place[longest] + 1) % dims[longest]
    return result.at[tuple(place)].set(high)


def spiked(drawn, rng, source, target, shards_of, factor):
    def block_of(dim):
        return (jnp.arange(drawn.shape[dim]) // (drawn.shape[dim] // shards_of)).reshape((-1,) + (1,) * (drawn.ndim - 1 - dim))

    near = jax.random.permutation(rng, shards_of)[block_of(target)]
    second = (block_of(target) + shards_of // 2) % shards_of
    return jnp.where((block_of(source) == near) | (block_of(source) == second), factor * drawn, drawn)


def block_scale(own_key, dims, cuts, low, high):
    factor_of, own = 1.0, jax.random.fold_in(own_key, 6)
    for position, parts in cuts:
        heights = jnp.exp(jax.random.uniform(jax.random.fold_in(own, position), (parts,), jnp.float32, low / len(cuts), high / len(cuts)))
        factor_of = factor_of * jnp.repeat(heights, dims[position] // parts).reshape([-1 if axis == position else 1 for axis in range(len(dims))])
    return factor_of


def scatter_about(own_key, extent, width, reach, shards=(), kind=jnp.bfloat16):
    entries = width * jax.random.normal(own_key, extent, jnp.float32)
    if shards:
        entries = entries * block_scale(own_key, extent, shards, -0.22, 0.18)
    return jnp.clip(entries, -reach, reach).astype(kind)


def heavy_noise(own_key, extent, spread, limit, pieces, heavy, kind=jnp.bfloat16):
    values = spread * jax.random.normal(own_key, extent, jnp.float32)
    if pieces:
        values = values * block_scale(own_key, extent, pieces, -0.22, 0.18)
    return jnp.clip(spiked(values, jax.random.fold_in(own_key, 3), *heavy), -limit, limit).astype(kind)


def setup_inputs(seed: int = 0) -> dict:
    key_list = jax.random.split(jax.random.key(seed), 4)
    return {
        "amplitudes": scatter_about(key_list[0], (NPB, ROWS, TILE), 1.0, 6.0, ((0, 128), (1, 4))),
        "integrals": heavy_noise(key_list[1], (NPB, TILE, W_AB), (NPB * TILE) ** -0.5, 0.03125, ((0, 128), (1, 4)), (0, 2, 128, 5.5)),
        "block_mask": touch_ends((jax.random.randint(key_list[2], (NPB,), 0, 4) < 3).astype(jnp.int32), jax.random.fold_in(key_list[2], 1), 0, 1),
    }


def reference(amplitudes, integrals, block_mask):
    def add_block(total, items):
        amp, integ, flag = items
        term = jnp.dot(amp, integ, preferred_element_type=jnp.float32)
        return total + flag.astype(jnp.float32) * term, None

    start = jnp.zeros((amplitudes.shape[1], integrals.shape[2]), jnp.float32)
    total, unused = lax.scan(add_block, start, (amplitudes, integrals, block_mask))
    return total
```

```python
import jax
import jax.numpy as jnp
from jax import lax
from jax.sharding import Mesh
from jax.sharding import PartitionSpec as P

NX, NZ, NYH, NYL, NC = 4, 16, 2, 2, 2
PAIR = ("x", "z", "yh")
OCC = ("yl", "core")
SWAP = [(0, 1), (1, 0)]


def per_device(amplitudes, integrals, block_mask):
    amp, integ = amplitudes[0], integrals[0]
    flag = block_mask[0].astype(jnp.float32)
    yl, core = lax.axis_index("yl"), lax.axis_index("core")
    half = amp.shape[1] // NYL
    quarter = half // NC
    rows = amp.shape[0]

    away = lax.dynamic_slice_in_dim(amp, (1 - yl) * half, half, axis=1)
    arrived = lax.ppermute(away, "yl", SWAP)
    integ_sib = lax.ppermute(integ, "core", SWAP)
    integ_lo = jnp.where(core == 0, integ, integ_sib)
    integ_hi = jnp.where(core == 0, integ_sib, integ)

    def product(rows_half):
        out = jnp.dot(rows_half[:, :quarter], integ_lo, preferred_element_type=jnp.float32)
        out += jnp.dot(rows_half[:, quarter:], integ_hi, preferred_element_type=jnp.float32)
        return flag * out

    home = product(lax.dynamic_slice_in_dim(amp, yl * half, half, axis=1))
    guest = product(arrived)
    low = jnp.where(yl == 0, home, guest)
    high = jnp.where(yl == 0, guest, home)
    both = jnp.stack([low, high]).reshape(2, rows, NYL, NC, -1)
    keep = jnp.where(core == 0, both[:, :, :, 0], both[:, :, :, 1])
    give = jnp.where(core == 0, both[:, :, :, 1], both[:, :, :, 0])
    got = lax.ppermute(give, "core", SWAP)
    even = jnp.where(core == 0, keep, got)
    odd = jnp.where(core == 0, got, keep)
    parts = jnp.stack([even, odd], axis=1)
    own = rows // (NZ * NYH)
    parts = parts.reshape(2, 2, NZ, NYH, own, NYL, -1).transpose(0, 1, 3, 5, 2, 4, 6)
    parts = parts.reshape(NX * NYH * NYL, NZ * own, -1)
    parts = lax.all_to_all(parts, ("x", "yh", "yl"), split_axis=0, concat_axis=0, tiled=True)
    plane = jnp.sum(parts, axis=0).reshape(NZ, own, -1)
    plane = lax.all_to_all(plane, "z", split_axis=0, concat_axis=0, tiled=True)
    return jnp.sum(plane, axis=0)


def solution(mesh):
    fine = Mesh(mesh.devices.reshape(NX, NZ, NYH, NYL, NC), PAIR + OCC)
    in_specs = (P(PAIR, OCC, None), P(PAIR, OCC, None), P(PAIR))
    return jax.shard_map(
        per_device, mesh=fine, in_specs=in_specs, out_specs=P(PAIR, OCC), check_vma=False
    )
```

```python
import jax
import jax.numpy as jnp
from jax import lax
from jax.experimental import pallas as pl
from jax.experimental.pallas import tpu as pltpu
from jax.sharding import Mesh
from jax.sharding import PartitionSpec as P

NX, NZ, NYH, NYL, NC = 4, 16, 2, 2, 2
PAIR = ("x", "z", "yh")
OCC = ("yl", "core")
SWAP = [(0, 1), (1, 0)]
VMEM = pl.BlockSpec(memory_space=pltpu.VMEM)
SMEM = pl.BlockSpec(memory_space=pltpu.SMEM)
HBM = pl.BlockSpec(memory_space=pltpu.HBM)
DMA = pltpu.SemaphoreType.DMA


def call(kernel, out_shape, in_specs, scratch=(), flops=0, moved=0):
    return pl.pallas_call(
        kernel,
        out_shape=out_shape,
        in_specs=in_specs,
        out_specs=jax.tree.map(lambda _: VMEM, out_shape),
        scratch_shapes=list(scratch),
        compiler_params=pltpu.CompilerParams(vmem_limit_bytes=32 * 2**20),
        cost_estimate=pl.CostEstimate(flops=flops, bytes_accessed=moved, transcendentals=0),
    )


def take_half(place, amp, out, token, sem):
    half = out.shape[1]
    offset = pl.multiple_of((1 - place[0]) * half, half)
    copy = pltpu.make_async_copy(amp.at[0, :, pl.ds(offset, half)], out, sem)
    copy.start()
    token[...] = jnp.zeros_like(token)
    copy.wait()


def part_columns(place, token, integ, own, others):
    del token
    width = own.shape[1] // NYL
    for out, side in ((own, place[1]), (others, 1 - place[1])):
        for yl in range(NYL):
            source = pl.ds(pl.multiple_of((yl * NC + side) * width, width), width)
            out[:, yl * width : (yl + 1) * width] = integ[:, source]


def spread(place, mask, a, own, sib, acc, out):
    quarter = own.shape[0]
    mine = a[:, pl.ds(pl.multiple_of(place[1] * quarter, quarter), quarter)]
    theirs = a[:, pl.ds(pl.multiple_of((1 - place[1]) * quarter, quarter), quarter)]
    total = jnp.dot(mine, own[...], preferred_element_type=jnp.float32)
    total += jnp.dot(theirs, sib[...], preferred_element_type=jnp.float32)
    acc[...] = mask[0].astype(jnp.float32) * total
    rows, width = out.shape[2:]
    own = rows // NZ
    for yh in range(NYH):
        for yl in range(NYL):
            for z in range(NZ):
                start = (z * NYH + yh) * own
                out[yh, yl, z * own : (z + 1) * own] = acc[start : start + own, yl * width : (yl + 1) * width]


def home_kernel(place, mask, amp, own_keep, sib_keep, own_give, sib_give, keep, give, half_ref, acc, sem):
    half = half_ref.shape[1]
    offset = pl.multiple_of(place[0] * half, half)
    copy = pltpu.make_async_copy(amp.at[0, :, pl.ds(offset, half)], half_ref, sem)
    copy.start()
    copy.wait()
    spread(place, mask, half_ref, own_give, sib_give, acc, give)
    spread(place, mask, half_ref, own_keep, sib_keep, acc, keep)


def guest_kernel(place, mask, arrived, own, sib, out, acc):
    spread(place, mask, arrived, own, sib, acc, out)


def assemble(place, keep_home, got_home, keep_guest, got_guest, out):
    yl, core = place[0], place[1]
    out[yl, core] = keep_home[...]
    out[yl, 1 - core] = got_home[...]
    out[1 - yl, core] = keep_guest[...]
    out[1 - yl, 1 - core] = got_guest[...]


def per_device(amplitudes, integrals, block_mask):
    rows, depth = amplitudes.shape[1:]
    half = depth // NYL
    own = rows // (NZ * NYH)
    width = integrals.shape[2] // (NYL * NC)
    place = jnp.stack([lax.axis_index("yl"), lax.axis_index("core")]).astype(jnp.int32)

    away, token = call(
        take_half,
        (
            jax.ShapeDtypeStruct((rows, half), jnp.bfloat16),
            jax.ShapeDtypeStruct((8, 128), jnp.float32),
        ),
        [SMEM, HBM],
        [DMA],
        moved=4 * rows * half,
    )(place, amplitudes)
    arrived = lax.ppermute(away, "yl", SWAP)
    depth_own, width_all = integrals.shape[1:]
    part = jax.ShapeDtypeStruct((depth_own, width_all // NC), jnp.bfloat16)
    own_keep, own_give = call(
        part_columns, (part, part), [SMEM, VMEM, VMEM], moved=2**21
    )(place, token, integrals[0])
    sib_keep = lax.ppermute(own_give, "core", SWAP)
    sib_give = lax.ppermute(own_keep, "core", SWAP)

    piece = jax.ShapeDtypeStruct((NYH, NYL, rows // NYH, width), jnp.float32)
    acc = pltpu.VMEM((rows, NYL * width), jnp.float32)
    work = 2 * rows * half * NYL * width
    keep_home, give_home = call(
        home_kernel,
        (piece, piece),
        [SMEM, SMEM, HBM] + [VMEM] * 4,
        [pltpu.VMEM((rows, half), jnp.bfloat16), acc, DMA],
        flops=1,
        moved=1,
    )(place, block_mask, amplitudes, own_keep, sib_keep, own_give, sib_give)
    got_home = lax.ppermute(give_home, "core", SWAP)

    def guest(own_columns, sib_columns):
        return call(
            guest_kernel,
            piece,
            [SMEM, SMEM, VMEM, VMEM, VMEM],
            [acc],
            flops=work,
            moved=2 * 2**20,
        )(place, block_mask, arrived, own_columns, sib_columns)

    got_guest = lax.ppermute(guest(own_give, sib_give), "core", SWAP)
    keep_guest = guest(own_keep, sib_keep)
    parts = call(
        assemble,
        jax.ShapeDtypeStruct((2, 2) + piece.shape, jnp.float32),
        [SMEM] + [VMEM] * 4,
        moved=2**21,
    )(place, keep_home, got_home, keep_guest, got_guest)
    parts = parts.reshape(NX * NYH * NYL, rows // NYH, width)
    parts = lax.all_to_all(parts, ("x", "yh", "yl"), split_axis=0, concat_axis=0, tiled=True)
    plane = jnp.sum(parts, axis=0).reshape(NZ, own, width)
    plane = lax.all_to_all(plane, "z", split_axis=0, concat_axis=0, tiled=True)
    return jnp.sum(plane, axis=0)


def solution(mesh):
    fine = Mesh(mesh.devices.reshape(NX, NZ, NYH, NYL, NC), PAIR + OCC)
    in_specs = (P(PAIR, OCC, None), P(PAIR, OCC, None), P(PAIR))
    return jax.shard_map(
        per_device, mesh=fine, in_specs=in_specs, out_specs=P(PAIR, OCC), check_vma=False
    )
```

```python
import jax
import jax.numpy as jnp
from jax import lax
from jax.experimental import pallas as pl
from jax.experimental.pallas import tpu as pltpu
from jax.sharding import Mesh
from jax.sharding import PartitionSpec as P

NX, NZ, NYH, NYL, NC = 4, 16, 2, 2, 2
PAIR = ("x", "z", "yh")
OCC = ("yl", "core")
SWAP = [(0, 1), (1, 0)]
VMEM = pl.BlockSpec(memory_space=pltpu.VMEM)
SMEM = pl.BlockSpec(memory_space=pltpu.SMEM)
HBM = pl.BlockSpec(memory_space=pltpu.HBM)
DMA = pltpu.SemaphoreType.DMA


def call(kernel, out_shape, in_specs, scratch=(), flops=0, moved=0):
    return pl.pallas_call(
        kernel,
        out_shape=out_shape,
        in_specs=in_specs,
        out_specs=jax.tree.map(lambda _: VMEM, out_shape),
        scratch_shapes=list(scratch),
        compiler_params=pltpu.CompilerParams(vmem_limit_bytes=32 * 2**20),
        cost_estimate=pl.CostEstimate(flops=flops, bytes_accessed=moved, transcendentals=0),
    )


def take_half(amp, out, token, sem):
    half = out.shape[1]
    offset = pl.multiple_of((1 - lax.axis_index("yl")) * half, half)
    copy = pltpu.make_async_copy(amp.at[0, :, pl.ds(offset, half)], out, sem)
    copy.start()
    token[...] = jnp.zeros_like(token)
    copy.wait()


def part_columns(token, integ, own, others):
    del token
    core = lax.axis_index("core")
    width = own.shape[1] // NYL
    for out, side in ((own, core), (others, 1 - core)):
        for yl in range(NYL):
            source = pl.ds(pl.multiple_of((yl * NC + side) * width, width), width)
            out[:, yl * width : (yl + 1) * width] = integ[:, source]


def spread(mask, a, columns, acc, out):
    acc[...] = mask[0].astype(jnp.float32) * jnp.dot(a[...], columns[...], preferred_element_type=jnp.float32)
    rows, width = out.shape[2:]
    own = rows // NZ
    for yh in range(NYH):
        for yl in range(NYL):
            for z in range(NZ):
                start = (z * NYH + yh) * own
                out[yh, yl, z * own : (z + 1) * own] = acc[start : start + own, yl * width : (yl + 1) * width]


def home_kernel(mask, amp, own_keep, sib_keep, own_give, sib_give, keep, give, keep_all, give_all, half_ref, acc, sem):
    half = half_ref.shape[1]
    yl, core = lax.axis_index("yl"), lax.axis_index("core")
    offset = pl.multiple_of(yl * half, half)
    copy = pltpu.make_async_copy(amp.at[0, :, pl.ds(offset, half)], half_ref, sem)
    copy.start()
    quarter = own_keep.shape[0]
    mine = pl.ds(pl.multiple_of(core * quarter, quarter), quarter)
    theirs = pl.ds(pl.multiple_of((1 - core) * quarter, quarter), quarter)
    keep_all[mine] = own_keep[...]
    keep_all[theirs] = sib_keep[...]
    give_all[mine] = own_give[...]
    give_all[theirs] = sib_give[...]
    copy.wait()
    spread(mask, half_ref, give_all, acc, give)
    spread(mask, half_ref, keep_all, acc, keep)


def give_kernel(mask, arrived, columns, out, acc):
    spread(mask, arrived, columns, acc, out)


def keep_kernel(mask, arrived, columns, keep_home, got_home, out, acc):
    yl, core = lax.axis_index("yl"), lax.axis_index("core")
    spread(mask, arrived, columns, acc, out.at[1 - yl, core])
    out[yl, core] = keep_home[...]
    out[yl, 1 - core] = got_home[...]


def per_device(amplitudes, integrals, block_mask):
    rows, depth = amplitudes.shape[1:]
    half = depth // NYL
    own = rows // (NZ * NYH)
    width = integrals.shape[2] // (NYL * NC)

    away, token = call(
        take_half,
        (
            jax.ShapeDtypeStruct((rows, half), jnp.bfloat16),
            jax.ShapeDtypeStruct((8, 128), jnp.float32),
        ),
        [HBM],
        [DMA],
        moved=4 * rows * half,
    )(amplitudes)
    arrived = lax.ppermute(away, "yl", SWAP)
    depth_own, width_all = integrals.shape[1:]
    part = jax.ShapeDtypeStruct((depth_own, width_all // NC), jnp.bfloat16)
    own_keep, own_give = call(
        part_columns, (part, part), [VMEM, VMEM], moved=2**21
    )(token, integrals[0])
    sib_keep = lax.ppermute(own_give, "core", SWAP)
    sib_give = lax.ppermute(own_keep, "core", SWAP)

    piece = jax.ShapeDtypeStruct((NYH, NYL, rows // NYH, width), jnp.float32)
    acc = pltpu.VMEM((rows, NYL * width), jnp.float32)
    columns = jax.ShapeDtypeStruct((half, width_all // NC), jnp.bfloat16)
    whole = jax.ShapeDtypeStruct((2, 2) + piece.shape, jnp.float32)
    work = 2 * rows * half * NYL * width
    keep_home, give_home, keep_columns, give_columns = call(
        home_kernel,
        (piece, piece, columns, columns),
        [SMEM, HBM] + [VMEM] * 4,
        [pltpu.VMEM((rows, half), jnp.bfloat16), acc, DMA],
        flops=1,
        moved=1,
    )(block_mask, amplitudes, own_keep, sib_keep, own_give, sib_give)
    got_home = lax.ppermute(give_home, "core", SWAP)

    give = call(give_kernel, piece, [SMEM, VMEM, VMEM], [acc], flops=work, moved=2**21)(
        block_mask, arrived, give_columns
    )
    got = lax.ppermute(give, "core", SWAP)
    parts = call(
        keep_kernel, whole, [SMEM] + [VMEM] * 4, [acc], flops=work, moved=2**22
    )(block_mask, arrived, keep_columns, keep_home, got_home)
    last = (1 - lax.axis_index("yl"), 1 - lax.axis_index("core")) + (0,) * 4
    parts = lax.dynamic_update_slice(parts, got[None, None], last)
    parts = parts.reshape(NX * NYH * NYL, rows // NYH, width)
    parts = lax.all_to_all(parts, ("x", "yh", "yl"), split_axis=0, concat_axis=0, tiled=True)
    plane = jnp.sum(parts, axis=0).reshape(NZ, own, width)
    plane = lax.all_to_all(plane, "z", split_axis=0, concat_axis=0, tiled=True)
    return jnp.sum(plane, axis=0)


def solution(mesh):
    fine = Mesh(mesh.devices.reshape(NX, NZ, NYH, NYL, NC), PAIR + OCC)
    in_specs = (P(PAIR, OCC, None), P(PAIR, OCC, None), P(PAIR))
    return jax.shard_map(
        per_device, mesh=fine, in_specs=in_specs, out_specs=P(PAIR, OCC), check_vma=False
    )
```

```python
import jax
import jax.numpy as jnp
from jax import lax
from jax.experimental import pallas as pl
from jax.experimental.pallas import tpu as pltpu
from jax.sharding import Mesh
from jax.sharding import PartitionSpec as P

NX, NZ, NYH, NYL, NC = 4, 16, 2, 2, 2
PAIR = ("x", "z", "yh")
OCC = ("yl", "core")
SWAP = [(0, 1), (1, 0)]
VMEM = pl.BlockSpec(memory_space=pltpu.VMEM)
SMEM = pl.BlockSpec(memory_space=pltpu.SMEM)
HBM = pl.BlockSpec(memory_space=pltpu.HBM)
DMA = pltpu.SemaphoreType.DMA


def call(kernel, out_shape, in_specs, scratch=(), flops=0, moved=0):
    return pl.pallas_call(
        kernel,
        out_shape=out_shape,
        in_specs=in_specs,
        out_specs=jax.tree.map(lambda _: VMEM, out_shape),
        scratch_shapes=list(scratch),
        compiler_params=pltpu.CompilerParams(vmem_limit_bytes=32 * 2**20),
        cost_estimate=pl.CostEstimate(flops=flops, bytes_accessed=moved, transcendentals=0),
    )


def take_half(amp, out, token, sem):
    half = out.shape[1]
    offset = pl.multiple_of((1 - lax.axis_index("yl")) * half, half)
    copy = pltpu.make_async_copy(amp.at[0, :, pl.ds(offset, half)], out, sem)
    copy.start()
    token[...] = jnp.zeros_like(token)
    copy.wait()


def take_late(sib_low, sib_high, early, away, out):
    del sib_low, sib_high, early
    out[...] = away[...]


def part_rows(token, integ, low, high):
    del token
    half = low.shape[0]
    low[...] = integ[:half]
    high[...] = integ[half:]


def spread(mask, a, columns, acc, out):
    acc[...] = mask[0].astype(jnp.float32) * jnp.dot(a[...], columns[...], preferred_element_type=jnp.float32)
    rows, width = out.shape[3:]
    own = rows // NZ
    for core in range(NC):
        for yh in range(NYH):
            for yl in range(NYL):
                left = (yl * NC + core) * width
                for z in range(NZ):
                    start = (z * NYH + yh) * own
                    out[core, yh, yl, z * own : (z + 1) * own] = acc[start : start + own, left : left + width]


def home_kernel(mask, amp, own_low, own_high, sib_low, sib_high, out, columns, half_ref, acc, sem):
    half = half_ref.shape[1]
    yl, core = lax.axis_index("yl"), lax.axis_index("core")
    offset = pl.multiple_of(yl * half, half)
    copy = pltpu.make_async_copy(amp.at[0, :, pl.ds(offset, half)], half_ref, sem)
    copy.start()
    depth = own_low.shape[0]
    for place, low, high in ((core, own_low, own_high), (1 - core, sib_low, sib_high)):
        first = pl.multiple_of(place * 2 * depth, 2 * depth)
        columns[pl.ds(first, depth)] = low[...]
        columns[pl.ds(first + depth, depth)] = high[...]
    copy.wait()
    spread(mask, half_ref, columns, acc, out)


def guest_kernel(mask, early, late, columns, home, out, acc):
    yl, core = lax.axis_index("yl"), lax.axis_index("core")
    out[yl] = home[...]

    @pl.when(core == 0)
    def _():
        spread(mask, early, columns, acc, out.at[1 - yl])

    @pl.when(core == 1)
    def _():
        spread(mask, late, columns, acc, out.at[1 - yl])


def per_device(amplitudes, integrals, block_mask):
    rows, depth = amplitudes.shape[1:]
    half = depth // NYL
    own = rows // (NZ * NYH)
    width = integrals.shape[2] // (NYL * NC)

    away, token = call(
        take_half,
        (
            jax.ShapeDtypeStruct((rows, half), jnp.bfloat16),
            jax.ShapeDtypeStruct((8, 128), jnp.float32),
        ),
        [HBM],
        [DMA],
        moved=4 * rows * half,
    )(amplitudes)
    early = lax.ppermute(away, OCC, [(0, 2), (2, 0)])
    depth_own, width_all = integrals.shape[1:]
    some_rows = jax.ShapeDtypeStruct((depth_own // 2, width_all), jnp.bfloat16)
    own_low, own_high = call(part_rows, (some_rows, some_rows), [VMEM, VMEM], moved=2**21)(
        token, integrals[0]
    )
    sib_low = lax.ppermute(own_low, "core", SWAP)
    sib_high = lax.ppermute(own_high, "core", SWAP)
    piece = jax.ShapeDtypeStruct((NC, NYH, NYL, rows // NYH, width), jnp.float32)
    acc = pltpu.VMEM((rows, width_all), jnp.float32)
    columns = jax.ShapeDtypeStruct((half, width_all), jnp.bfloat16)
    home, all_columns = call(
        home_kernel,
        (piece, columns),
        [SMEM, HBM] + [VMEM] * 4,
        [pltpu.VMEM((rows, half), jnp.bfloat16), acc, DMA],
        flops=1,
        moved=1,
    )(block_mask, amplitudes, own_low, own_high, sib_low, sib_high)
    away_late = call(
        take_late, jax.ShapeDtypeStruct((rows, half), jnp.bfloat16), [VMEM] * 4, moved=1
    )(sib_low, sib_high, early, away)
    late = lax.ppermute(away_late, OCC, [(1, 3), (3, 1)])

    parts = call(
        guest_kernel,
        jax.ShapeDtypeStruct((2,) + piece.shape, jnp.float32),
        [SMEM] + [VMEM] * 4,
        [acc],
        flops=2 * rows * half * width_all,
        moved=2**22,
    )(block_mask, early, late, all_columns, home)
    parts = parts.reshape(NX * NYH * NYL, rows // NYH, width)
    parts = lax.all_to_all(parts, ("x", "yh", "yl"), split_axis=0, concat_axis=0, tiled=True)
    plane = jnp.sum(parts, axis=0).reshape(NZ, own, width)
    plane = lax.all_to_all(plane, "z", split_axis=0, concat_axis=0, tiled=True)
    block = jnp.sum(plane, axis=0)
    swap = [((h * 2 + b) * NC + c, (h * 2 + c) * NC + b) for h in range(2) for b in range(2) for c in range(NC)]
    return lax.ppermute(block, ("x", "core"), swap)


def solution(mesh):
    fine = Mesh(mesh.devices.reshape(NX, NZ, NYH, NYL, NC), PAIR + OCC)
    in_specs = (P(PAIR, OCC, None), P(PAIR, OCC, None), P(PAIR))
    return jax.shard_map(
        per_device, mesh=fine, in_specs=in_specs, out_specs=P(PAIR, OCC), check_vma=False
    )
```

```python
import jax
import jax.numpy as jnp
from jax import lax
from jax.experimental import pallas as pl
from jax.experimental.pallas import tpu as pltpu
from jax.sharding import Mesh
from jax.sharding import PartitionSpec as P

NX, NZ, NYH, NYL, NC = 4, 16, 2, 2, 2
PAIR = ("x", "z", "yh")
OCC = ("yl", "core")
SWAP = [(0, 1), (1, 0)]
VMEM = pl.BlockSpec(memory_space=pltpu.VMEM)
SMEM = pl.BlockSpec(memory_space=pltpu.SMEM)
HBM = pl.BlockSpec(memory_space=pltpu.HBM)
DMA = pltpu.SemaphoreType.DMA


def call(kernel, out_shape, in_specs, scratch=(), flops=0, moved=0, limit=32):
    return pl.pallas_call(
        kernel,
        out_shape=out_shape,
        in_specs=in_specs,
        out_specs=jax.tree.map(lambda _: VMEM, out_shape),
        scratch_shapes=list(scratch),
        compiler_params=pltpu.CompilerParams(vmem_limit_bytes=limit * 2**20),
        cost_estimate=pl.CostEstimate(flops=flops, bytes_accessed=moved, transcendentals=0),
    )


def take_half(amp, out, token, sem):
    rows, half = out.shape
    columns = pl.ds(pl.multiple_of((1 - lax.axis_index("yl")) * half, half), half)
    copies = []
    for i in range(4):
        some = pl.ds(i * rows // 4, rows // 4)
        copies.append(pltpu.make_async_copy(amp.at[0, some, columns], out.at[some], sem.at[i]))
    for copy in copies:
        copy.start()
    token[...] = jnp.zeros_like(token)
    for copy in copies:
        copy.wait()


def take_late(sib_low, sib_high, early, away, out):
    del sib_low, sib_high, early
    out[...] = away[...]


def part_rows(token, integ, low, high):
    del token
    half = low.shape[0]
    low[...] = integ[:half]
    high[...] = integ[half:]


def spread(mask, a, columns, acc, out):
    acc[...] = mask[0].astype(jnp.float32) * jnp.dot(a[...], columns[...], preferred_element_type=jnp.float32)
    rows, width = out.shape[3:]
    own = rows // NZ
    for core in range(NC):
        for yh in range(NYH):
            for yl in range(NYL):
                left = (yl * NC + core) * width
                for z in range(NZ):
                    start = (z * NYH + yh) * own
                    out[core, yh, yl, z * own : (z + 1) * own] = acc[start : start + own, left : left + width]


def home_kernel(mask, amp, own_low, own_high, sib_low, sib_high, out, columns, half_ref, acc, sem):
    half = half_ref.shape[1]
    yl, core = lax.axis_index("yl"), lax.axis_index("core")
    offset = pl.multiple_of(yl * half, half)
    copy = pltpu.make_async_copy(amp.at[0, :, pl.ds(offset, half)], half_ref, sem)
    copy.start()
    depth = own_low.shape[0]
    for place, low, high in ((core, own_low, own_high), (1 - core, sib_low, sib_high)):
        first = pl.multiple_of(place * 2 * depth, 2 * depth)
        columns[pl.ds(first, depth)] = low[...]
        columns[pl.ds(first + depth, depth)] = high[...]
    copy.wait()
    spread(mask, half_ref, columns, acc, out)


def guest_kernel(mask, early, late, columns, home, out, acc):
    yl, core = lax.axis_index("yl"), lax.axis_index("core")
    out[yl] = home[...]

    @pl.when(core == 0)
    def _():
        spread(mask, early, columns, acc, out.at[1 - yl])

    @pl.when(core == 1)
    def _():
        spread(mask, late, columns, acc, out.at[1 - yl])


def per_device(amplitudes, integrals, block_mask):
    rows, depth = amplitudes.shape[1:]
    half = depth // NYL
    own = rows // (NZ * NYH)
    width = integrals.shape[2] // (NYL * NC)

    away, token = call(
        take_half,
        (
            jax.ShapeDtypeStruct((rows, half), jnp.bfloat16),
            jax.ShapeDtypeStruct((8, 128), jnp.float32),
        ),
        [HBM],
        [pltpu.SemaphoreType.DMA((4,))],
        moved=4 * rows * half,
        limit=52,
    )(amplitudes)
    early = lax.ppermute(away, OCC, [(0, 2), (2, 0)])
    depth_own, width_all = integrals.shape[1:]
    some_rows = jax.ShapeDtypeStruct((depth_own // 2, width_all), jnp.bfloat16)
    own_low, own_high = call(part_rows, (some_rows, some_rows), [VMEM, VMEM], moved=2**21)(
        token, integrals[0]
    )
    sib_low = lax.ppermute(own_low, "core", SWAP)
    sib_high = lax.ppermute(own_high, "core", SWAP)
    piece = jax.ShapeDtypeStruct((NC, NYH, NYL, rows // NYH, width), jnp.float32)
    acc = pltpu.VMEM((rows, width_all), jnp.float32)
    columns = jax.ShapeDtypeStruct((half, width_all), jnp.bfloat16)
    home, all_columns = call(
        home_kernel,
        (piece, columns),
        [SMEM, HBM] + [VMEM] * 4,
        [pltpu.VMEM((rows, half), jnp.bfloat16), acc, DMA],
        flops=1,
        moved=1,
    )(block_mask, amplitudes, own_low, own_high, sib_low, sib_high)
    away_late = call(
        take_late, jax.ShapeDtypeStruct((rows, half), jnp.bfloat16), [VMEM] * 4, moved=1
    )(sib_low, sib_high, early, away)
    late = lax.ppermute(away_late, OCC, [(1, 3), (3, 1)])

    parts = call(
        guest_kernel,
        jax.ShapeDtypeStruct((2,) + piece.shape, jnp.float32),
        [SMEM] + [VMEM] * 4,
        [acc],
        flops=2 * rows * half * width_all,
        moved=2**22,
    )(block_mask, early, late, all_columns, home)
    parts = parts.reshape(NX * NYH * NYL, rows // NYH, width)
    parts = lax.all_to_all(parts, ("x", "yh", "yl"), split_axis=0, concat_axis=0, tiled=True)
    plane = jnp.sum(parts, axis=0).reshape(NZ, own, width)
    plane = lax.all_to_all(plane, "z", split_axis=0, concat_axis=0, tiled=True)
    block = jnp.sum(plane, axis=0)
    swap = [((h * 2 + b) * NC + c, (h * 2 + c) * NC + b) for h in range(2) for b in range(2) for c in range(NC)]
    return lax.ppermute(block, ("x", "core"), swap)


def solution(mesh):
    fine = Mesh(mesh.devices.reshape(NX, NZ, NYH, NYL, NC), PAIR + OCC)
    in_specs = (P(PAIR, OCC, None), P(PAIR, OCC, None), P(PAIR))
    return jax.shard_map(
        per_device, mesh=fine, in_specs=in_specs, out_specs=P(PAIR, OCC), check_vma=False
    )
```

```python
import jax
import jax.numpy as jnp
from jax import lax
from jax.experimental import pallas as pl
from jax.experimental.pallas import tpu as pltpu
from jax.sharding import Mesh
from jax.sharding import PartitionSpec as P

NX, NZ, NYH, NYL, NC = 4, 16, 2, 2, 2
PAIR = ("x", "z", "yh")
OCC = ("yl", "core")
SWAP = [(0, 1), (1, 0)]
VMEM = pl.BlockSpec(memory_space=pltpu.VMEM)
SMEM = pl.BlockSpec(memory_space=pltpu.SMEM)
HBM = pl.BlockSpec(memory_space=pltpu.HBM)
DMA = pltpu.SemaphoreType.DMA


def call(kernel, out_shape, in_specs, scratch=(), flops=0, moved=0, limit=32):
    return pl.pallas_call(
        kernel,
        out_shape=out_shape,
        in_specs=in_specs,
        out_specs=jax.tree.map(lambda _: VMEM, out_shape),
        scratch_shapes=list(scratch),
        compiler_params=pltpu.CompilerParams(vmem_limit_bytes=limit * 2**20),
        cost_estimate=pl.CostEstimate(flops=flops, bytes_accessed=moved, transcendentals=0),
    )


def take_half(amp, out, token, sem):
    rows, half = out.shape
    columns = pl.ds(pl.multiple_of((1 - lax.axis_index("yl")) * half, half), half)
    copies = []
    for i in range(4):
        some = pl.ds(i * rows // 4, rows // 4)
        copies.append(pltpu.make_async_copy(amp.at[0, some, columns], out.at[some], sem.at[i]))
    for copy in copies:
        copy.start()
    token[...] = jnp.zeros_like(token)
    for copy in copies:
        copy.wait()


def take_late(sib_low, sib_high, early, away, out):
    del sib_low, sib_high, early
    out[...] = away[...]


def part_rows(token, integ, low, high, sem):
    del token
    cut = low.shape[0]
    copies = [
        pltpu.make_async_copy(integ.at[0, pl.ds(i * cut, cut)], out, sem.at[i]) for i, out in enumerate((low, high))
    ]
    for copy in copies:
        copy.start()
    for copy in copies:
        copy.wait()


def spread(mask, a, columns, acc, out):
    acc[...] = mask[0].astype(jnp.float32) * jnp.dot(a[...], columns[...], preferred_element_type=jnp.float32)
    rows, width = out.shape[3:]
    own = rows // NZ
    for core in range(NC):
        for yh in range(NYH):
            for yl in range(NYL):
                left = (yl * NC + core) * width
                for z in range(NZ):
                    start = (z * NYH + yh) * own
                    out[core, yh, yl, z * own : (z + 1) * own] = acc[start : start + own, left : left + width]


def home_kernel(mask, amp, own_low, own_high, sib_low, sib_high, out, columns, half_ref, acc, sem):
    half = half_ref.shape[1]
    yl, core = lax.axis_index("yl"), lax.axis_index("core")
    offset = pl.multiple_of(yl * half, half)
    copy = pltpu.make_async_copy(amp.at[0, :, pl.ds(offset, half)], half_ref, sem)
    copy.start()
    depth = own_low.shape[0]
    for place, low, high in ((core, own_low, own_high), (1 - core, sib_low, sib_high)):
        first = pl.multiple_of(place * 2 * depth, 2 * depth)
        columns[pl.ds(first, depth)] = low[...]
        columns[pl.ds(first + depth, depth)] = high[...]
    copy.wait()
    spread(mask, half_ref, columns, acc, out.at[yl])


def guest_kernel(mask, early, late, columns, out, acc):
    core = lax.axis_index("core")

    @pl.when(core == 0)
    def _():
        spread(mask, early, columns, acc, out)

    @pl.when(core == 1)
    def _():
        spread(mask, late, columns, acc, out)


def per_device(amplitudes, integrals, block_mask):
    rows, depth = amplitudes.shape[1:]
    half = depth // NYL
    own = rows // (NZ * NYH)
    width = integrals.shape[2] // (NYL * NC)

    away, token = call(
        take_half,
        (
            jax.ShapeDtypeStruct((rows, half), jnp.bfloat16),
            jax.ShapeDtypeStruct((8, 128), jnp.float32),
        ),
        [HBM],
        [pltpu.SemaphoreType.DMA((4,))],
        moved=4 * rows * half,
        limit=52,
    )(amplitudes)
    early = lax.ppermute(away, OCC, [(0, 2), (2, 0)])
    depth_own, width_all = integrals.shape[1:]
    some_rows = jax.ShapeDtypeStruct((depth_own // 2, width_all), jnp.bfloat16)
    own_low, own_high = call(
        part_rows, (some_rows, some_rows), [VMEM, HBM], [pltpu.SemaphoreType.DMA((2,))], moved=2**21, limit=52
    )(token, integrals)
    sib_low = lax.ppermute(own_low, "core", SWAP)
    sib_high = lax.ppermute(own_high, "core", SWAP)
    piece = jax.ShapeDtypeStruct((NC, NYH, NYL, rows // NYH, width), jnp.float32)
    acc = pltpu.VMEM((rows, width_all), jnp.float32)
    columns = jax.ShapeDtypeStruct((half, width_all), jnp.bfloat16)
    whole = jax.ShapeDtypeStruct((2,) + piece.shape, jnp.float32)
    parts, all_columns = call(
        home_kernel,
        (whole, columns),
        [SMEM, HBM] + [VMEM] * 4,
        [pltpu.VMEM((rows, half), jnp.bfloat16), acc, DMA],
        flops=1,
        moved=1,
    )(block_mask, amplitudes, own_low, own_high, sib_low, sib_high)
    away_late = call(
        take_late, jax.ShapeDtypeStruct((rows, half), jnp.bfloat16), [VMEM] * 4, moved=1
    )(sib_low, sib_high, early, away)
    late = lax.ppermute(away_late, OCC, [(1, 3), (3, 1)])

    guest = call(
        guest_kernel,
        piece,
        [SMEM] + [VMEM] * 3,
        [acc],
        flops=2 * rows * half * width_all,
        moved=2**22,
    )(block_mask, early, late, all_columns)
    parts = lax.dynamic_update_slice(parts, guest[None], (1 - lax.axis_index("yl"),) + (0,) * 5)
    parts = parts.reshape(NX * NYH * NYL, rows // NYH, width)
    parts = lax.all_to_all(parts, ("x", "yh", "yl"), split_axis=0, concat_axis=0, tiled=True)
    plane = jnp.sum(parts, axis=0).reshape(NZ, own, width)
    plane = lax.all_to_all(plane, "z", split_axis=0, concat_axis=0, tiled=True)
    block = jnp.sum(plane, axis=0)
    swap = [((h * 2 + b) * NC + c, (h * 2 + c) * NC + b) for h in range(2) for b in range(2) for c in range(NC)]
    return lax.ppermute(block, ("x", "core"), swap)


def solution(mesh):
    fine = Mesh(mesh.devices.reshape(NX, NZ, NYH, NYL, NC), PAIR + OCC)
    in_specs = (P(PAIR, OCC, None), P(PAIR, OCC, None), P(PAIR))
    return jax.shard_map(
        per_device, mesh=fine, in_specs=in_specs, out_specs=P(PAIR, OCC), check_vma=False
    )
```

```python
import jax
import jax.numpy as jnp
from jax import lax
from jax.experimental import pallas as pl
from jax.experimental.pallas import tpu as pltpu
from jax.sharding import Mesh
from jax.sharding import PartitionSpec as P

NX, NZ, NYH, NYL, NC = 4, 16, 2, 2, 2
PAIR = ("x", "z", "yh")
OCC = ("yl", "core")
SWAP = [(0, 1), (1, 0)]
VMEM = pl.BlockSpec(memory_space=pltpu.VMEM)
SMEM = pl.BlockSpec(memory_space=pltpu.SMEM)
HBM = pl.BlockSpec(memory_space=pltpu.HBM)
DMA = pltpu.SemaphoreType.DMA


def call(kernel, out_shape, in_specs, scratch=(), flops=0, moved=0, limit=32):
    return pl.pallas_call(
        kernel,
        out_shape=out_shape,
        in_specs=in_specs,
        out_specs=jax.tree.map(lambda _: VMEM, out_shape),
        scratch_shapes=list(scratch),
        compiler_params=pltpu.CompilerParams(vmem_limit_bytes=limit * 2**20),
        cost_estimate=pl.CostEstimate(flops=flops, bytes_accessed=moved, transcendentals=0),
    )


def take_half(amp, out, token, sem):
    rows, half = out.shape
    columns = pl.ds(pl.multiple_of((1 - lax.axis_index("yl")) * half, half), half)
    copies = []
    for i in range(4):
        some = pl.ds(i * rows // 4, rows // 4)
        copies.append(pltpu.make_async_copy(amp.at[0, some, columns], out.at[some], sem.at[i]))
    for copy in copies:
        copy.start()
    token[...] = jnp.zeros_like(token)
    for copy in copies:
        copy.wait()


def take_late(sib_low, sib_high, early, away, out):
    del sib_low, sib_high, early
    out[...] = away[...]


def part_rows(token, integ, low, high):
    del token
    half = low.shape[0]
    low[...] = integ[:half]
    high[...] = integ[half:]


def spread(mask, a, columns, acc, out):
    acc[...] = mask[0].astype(jnp.float32) * jnp.dot(a[...], columns[...], preferred_element_type=jnp.float32)
    rows, width = out.shape[3:]
    own = rows // NZ
    for core in range(NC):
        for yh in range(NYH):
            for yl in range(NYL):
                left = (yl * NC + core) * width
                for z in range(NZ):
                    start = (z * NYH + yh) * own
                    out[core, yh, yl, z * own : (z + 1) * own] = acc[start : start + own, left : left + width]


def home_kernel(mask, amp, own_low, own_high, sib_low, sib_high, out, columns, half_ref, acc, sem):
    half = half_ref.shape[1]
    yl, core = lax.axis_index("yl"), lax.axis_index("core")
    offset = pl.multiple_of(yl * half, half)
    copy = pltpu.make_async_copy(amp.at[0, :, pl.ds(offset, half)], half_ref, sem)
    copy.start()
    depth = own_low.shape[0]
    for place, low, high in ((core, own_low, own_high), (1 - core, sib_low, sib_high)):
        first = pl.multiple_of(place * 2 * depth, 2 * depth)
        columns[pl.ds(first, depth)] = low[...]
        columns[pl.ds(first + depth, depth)] = high[...]
    copy.wait()
    spread(mask, half_ref, columns, acc, out.at[yl])


def guest_kernel(mask, early, late, columns, out, acc):
    core = lax.axis_index("core")

    @pl.when(core == 0)
    def _():
        spread(mask, early, columns, acc, out)

    @pl.when(core == 1)
    def _():
        spread(mask, late, columns, acc, out)


def per_device(amplitudes, integrals, block_mask):
    rows, depth = amplitudes.shape[1:]
    half = depth // NYL
    own = rows // (NZ * NYH)
    width = integrals.shape[2] // (NYL * NC)

    away, token = call(
        take_half,
        (
            jax.ShapeDtypeStruct((rows, half), jnp.bfloat16),
            jax.ShapeDtypeStruct((8, 128), jnp.float32),
        ),
        [HBM],
        [pltpu.SemaphoreType.DMA((4,))],
        moved=4 * rows * half,
        limit=52,
    )(amplitudes)
    early = lax.ppermute(away, OCC, [(0, 2), (2, 0)])
    depth_own, width_all = integrals.shape[1:]
    some_rows = jax.ShapeDtypeStruct((depth_own // 2, width_all), jnp.bfloat16)
    own_low, own_high = call(part_rows, (some_rows, some_rows), [VMEM, VMEM], moved=2**21)(
        token, integrals[0]
    )
    sib_low = lax.ppermute(own_low, "core", SWAP)
    sib_high = lax.ppermute(own_high, "core", SWAP)
    piece = jax.ShapeDtypeStruct((NC, NYH, NYL, rows // NYH, width), jnp.float32)
    acc = pltpu.VMEM((rows, width_all), jnp.float32)
    columns = jax.ShapeDtypeStruct((half, width_all), jnp.bfloat16)
    whole = jax.ShapeDtypeStruct((2,) + piece.shape, jnp.float32)
    parts, all_columns = call(
        home_kernel,
        (whole, columns),
        [SMEM, HBM] + [VMEM] * 4,
        [pltpu.VMEM((rows, half), jnp.bfloat16), acc, DMA],
        flops=1,
        moved=1,
    )(block_mask, amplitudes, own_low, own_high, sib_low, sib_high)
    away_late = call(
        take_late, jax.ShapeDtypeStruct((rows, half), jnp.bfloat16), [VMEM] * 4, moved=1
    )(sib_low, sib_high, early, away)
    late = lax.ppermute(away_late, OCC, [(1, 3), (3, 1)])

    guest = call(
        guest_kernel,
        piece,
        [SMEM] + [VMEM] * 3,
        [acc],
        flops=2 * rows * half * width_all,
        moved=2**22,
    )(block_mask, early, late, all_columns)
    parts = lax.dynamic_update_slice(parts, guest[None], (1 - lax.axis_index("yl"),) + (0,) * 5)
    parts = parts.reshape(NX * NYH * NYL, rows // NYH, width)
    parts = lax.all_to_all(parts, ("x", "yh", "yl"), split_axis=0, concat_axis=0, tiled=True)
    plane = jnp.sum(parts, axis=0).reshape(NZ, own, width)
    plane = lax.all_to_all(plane, "z", split_axis=0, concat_axis=0, tiled=True)
    block = jnp.sum(plane, axis=0)
    swap = [((h * 2 + b) * NC + c, (h * 2 + c) * NC + b) for h in range(2) for b in range(2) for c in range(NC)]
    return lax.ppermute(block, ("x", "core"), swap)


def solution(mesh):
    fine = Mesh(mesh.devices.reshape(NX, NZ, NYH, NYL, NC), PAIR + OCC)
    in_specs = (P(PAIR, OCC, None), P(PAIR, OCC, None), P(PAIR))
    return jax.shard_map(
        per_device, mesh=fine, in_specs=in_specs, out_specs=P(PAIR, OCC), check_vma=False
    )
```
